512 devices in a mesh: traj: 32 (over x, y), cand: 16 (over z, core).
Axes of the slice: x: 4, y: 8, z: 8, core: 2. Of those that a mesh axis runs over, the one named last changes fastest.
Arguments:
- state: float32 [4096, 256], P('traj'), may hold values from -6 to 6
- target: float32 [4096, 256], P('traj'), may hold values from -6 to 6
- coeffs: bfloat16 [33280, 256], P('cand'), may hold values from -6 to 6
- pairs: int32 [2, 33280], P(None, 'cand'), may hold values from 0 to 256, as said below
- mask: int32 [33280, 256], P('cand'), may hold values 0 or 1
Outputs:
- slope: float32 [4096, 256], P('traj')
- new_coeffs: bfloat16 [33280, 256], P('cand')
The draws below stay inside these ranges and needn't reach their ends.
Inputs may be any that keep to these rules, and one draw needn't show every extreme that they name: Each column holds a pair pairs[0, c] <= pairs[1, c]; index 256 stands for the constant 1; no pair repeats before every pair has appeared.
All inputs are finite; a program needn't handle non-finite values. No bound on the sum of `mask` on one device may be relied on, other than what follows from the above.
Results may differ from the reference program's by a relative error of at most 0.014.
Values may be sent and summed in bfloat16 or wider, within the bound.
No kernel may reach another device: no remote copies, remote signals or barrier semaphores. Data moves between devices by JAX's collectives and lax.ppermute only.
A program may use at most 64 MiB of HBM per device.

```python
import math
import jax
import jax.numpy as jnp
import numpy as np
from jax import lax

M = 256
CANDS = 33280
S_DEV = 128
SEGMENTS = 4096
N_TRAJ = 32


def draw_pairs(key, part):
    side = M + 1
    upper = np.triu_indices(side)
    first = jnp.asarray(upper[0].astype(np.int32))
    second = jnp.asarray(upper[1].astype(np.int32))
    valid = side * (side + 1) // 2
    order = jax.random.permutation(key, valid).astype(jnp.int32)
    picked = order[jnp.arange(CANDS, dtype=jnp.int32) % valid]
    return jnp.stack([first[picked], second[picked]]).astype(jnp.int32)


def place_ends(entries, stream_key, low, top_value):
    longest = entries.shape.index(max(entries.shape))
    spots = []
    for shift in (0, 1):
        where = [jax.random.randint(jax.random.fold_in(stream_key, axis), (), 0, length) for axis, length in enumerate(entries.shape)]
        where[longest] = (where[longest] + shift) % entries.shape[longest]
        spots.append(tuple(where))
    return entries.at[spots[0]].set(low).at[spots[1]].set(top_value)


def strengthened(drawn, stream_key, source, target, parts, factor):
    owner, partner = [(jnp.arange(drawn.shape[position]) // (drawn.shape[position] // parts)).reshape([-1 if axis == position else 1 for axis in range(drawn.ndim)]) for position in (source, target)]
    chosen = jax.random.permutation(stream_key, parts)[partner]
    strong = (owner == chosen) | (owner == (partner + parts // 2) % parts)
    return jnp.where(strong, factor * drawn, drawn)


def levels(stream_key, dims, shards, least, largest):
    level, own = 1.0, jax.random.fold_in(stream_key, 6)
    for position, blocks in shards:
        heights = jnp.exp(jax.random.uniform(jax.random.fold_in(own, position), (blocks,), jnp.float32, least / len(shards), largest / len(shards)))
        level = level * jnp.repeat(heights, dims[position] // blocks).reshape([-1 if axis == position else 1 for axis in range(len(dims))])
    return level


def noise(stream_key, dims, width, limit, split=(), kind=jnp.bfloat16):
    values = width * jax.random.normal(stream_key, dims, jnp.float32)
    if split:
        values = values * levels(stream_key, dims, split, -0.22, 0.18)
    return jnp.clip(values, -limit, limit).astype(kind)


def bell_draw_with(key, extent, scale, most, shards, heavy, kind=jnp.bfloat16):
    values = scale * jax.random.normal(key, extent, jnp.float32)
    if shards:
        values = values * levels(key, extent, shards, -0.22, 0.18)
    return jnp.clip(strengthened(values, jax.random.fold_in(key, 3), *heavy), -most, most).astype(kind)


def setup_inputs(seed: int = 0) -> dict:
    streams_of = jax.random.split(jax.random.key(seed), 6)
    state = noise(streams_of[0], (SEGMENTS, M), 2.0, 6.0, ((0, 32),), jnp.float32)
    target = bell_draw_with(streams_of[1], (SEGMENTS, M), 1.0, 6.0, ((0, 32),), (0, 1, 32, 2.75), jnp.float32)
    coeffs = noise(streams_of[2], (CANDS, M), 1.0, 6.0, ((0, 16),))
    pairs = draw_pairs(jax.random.fold_in(streams_of[5], 71), 0)
    mask = place_ends((jax.random.randint(streams_of[4], (CANDS, M), 0, 4) < 3).astype(jnp.int32), jax.random.fold_in(streams_of[4], 1), 0, 1)
    return dict(state=state, target=target, coeffs=coeffs, pairs=pairs, mask=mask)


step_dt = 0.25

def widen(value):
    return lax.optimization_barrier(value.astype(jnp.bfloat16)).astype(jnp.float32)

def reference(state, target, coeffs, pairs, mask):
    left = pairs[0]
    right = pairs[1]
    scale = 1.0 / math.sqrt(CANDS)
    highest = lax.Precision.HIGHEST
    modes = jnp.arange(M, dtype=jnp.int32)
    jac = jnp.concatenate([left[:, None] == modes[None, :], right[:, None] == modes[None, :]], 0).astype(jnp.float32)
    coef_wide = coeffs.astype(jnp.float32)
    coef_trans = jnp.transpose(coef_wide)
    segments = S_DEV * N_TRAJ

    def library(y):
        z = jnp.concatenate([y, jnp.ones((y.shape[0], 1), y.dtype)], 1)
        left_vals = z[:, left]
        right_vals = z[:, right]
        return (widen(left_vals * right_vals), left_vals, right_vals)

    def derive(theta):
        return jnp.dot(theta, coef_wide, precision=highest) * scale

    def pullback(cot, left_vals, right_vals):
        hidden = jnp.dot(widen(cot), coef_trans, precision=highest) * scale
        joined = widen(jnp.concatenate([hidden * right_vals, hidden * left_vals], 1))
        return jnp.dot(joined, jac, precision=highest)

    def block(total, operands):
        start, observed = operands
        th1, l1, r1 = library(start)
        k1 = derive(th1)
        th2, l2, r2 = library(start + 0.5 * step_dt * k1)
        k2 = derive(th2)
        th3, l3, r3 = library(start + 0.5 * step_dt * k2)
        k3 = derive(th3)
        th4, l4, r4 = library(start + step_dt * k3)
        k4 = derive(th4)
        slope = (k1 + 2.0 * k2 + 2.0 * k3 + k4) / 6.0
        cot = (start + step_dt * slope - observed) / segments
        g4 = step_dt / 6.0 * cot
        c4 = pullback(g4, l4, r4)
        g3 = step_dt / 3.0 * cot + step_dt * c4
        c3 = pullback(g3, l3, r3)
        g2 = step_dt / 3.0 * cot + 0.5 * step_dt * c3
        c2 = pullback(g2, l2, r2)
        g1 = step_dt / 6.0 * cot + 0.5 * step_dt * c2
        thetas = jnp.concatenate([th1, th2, th3, th4], 0)
        cots = widen(jnp.concatenate([g1, g2, g3, g4], 0))
        grad = jnp.dot(jnp.transpose(thetas), cots, precision=highest) * scale
        return (total + grad, slope)
    grads, slopes = lax.scan(block, jnp.zeros((CANDS, M), state.dtype), (state.reshape(N_TRAJ, S_DEV, M), target.reshape(N_TRAJ, S_DEV, M)))
    rate = 0.5 * math.sqrt(segments * CANDS) / step_dt
    fresh = (mask.astype(grads.dtype) * (coef_wide - rate * grads)).astype(jnp.bfloat16)
    return (slopes.reshape(segments, M), fresh)
```

```python
import functools
import math

import jax
import jax.numpy as jnp
from jax import lax
from jax.experimental import pallas as pl
from jax.experimental.pallas import tpu as pltpu
from jax.sharding import PartitionSpec as P

DT = 0.25
NT = (((1,), (1,)), ((), ()))
CHUNK = 1664
FULL = pl.BlockSpec(memory_space=pltpu.VMEM)


def chain_kernel(
    scale,
    segments,
    state_ref,
    target_ref,
    left_ref,
    right_ref,
    w_hbm,
    hot_hbm,
    out_ref,
    w_ref,
    hot_ref,
    zl_ref,
    zr_ref,
    u_ref,
    keep_ref,
    sems,
):
    rows, modes = state_ref.shape
    total = w_ref.shape[0]
    groups = modes // 64

    def fetch(start):
        at = pl.ds(start, CHUNK)
        return pltpu.make_async_copy(w_hbm.at[at], w_ref.at[at], sems.at[start // CHUNK])

    fetches = [fetch(start) for start in range(0, total, CHUNK)]
    for copy in fetches:
        copy.start()
    hot_copy = pltpu.make_async_copy(hot_hbm, hot_ref, sems.at[total // CHUNK])
    hot_copy.start()
    state = state_ref[...]

    def derive(y, s, waits=None):
        halves = [y[:, j : j + 128] for j in range(0, modes, 128)]

        def pick(index):
            index = jnp.broadcast_to(index, (rows, 128))
            lane = index & 127
            value = jnp.ones((rows, 128), jnp.float32)
            for j in reversed(range(len(halves))):
                value = jnp.where(index < 128 * (j + 1), jnp.take_along_axis(halves[j], lane, axis=1), value)
            return value

        acc = jnp.zeros((rows, modes), jnp.float32)
        for start in range(0, total, CHUNK):
            parts = []
            for j in range(start, start + CHUNK, 128):
                zl, zr = pick(left_ref[0:1, j : j + 128]), pick(right_ref[0:1, j : j + 128])
                zl_ref[s, :, j : j + 128] = zl
                zr_ref[s, :, j : j + 128] = zr
                parts.append((zl * zr).astype(jnp.bfloat16))
            theta = jnp.concatenate(parts, axis=1)
            if waits is not None:
                waits[start // CHUNK].wait()
            acc = acc + jnp.dot(theta, w_ref[start : start + CHUNK, :], preferred_element_type=jnp.float32)
        return scale * acc

    def pull(g, s):
        g16 = g.astype(jnp.bfloat16)
        for start in range(0, total, CHUNK):
            w = w_ref[start : start + CHUNK, :]
            h = scale * lax.dot_general(g16, w, NT, preferred_element_type=jnp.float32)
            for j in range(0, CHUNK, 128):
                at = slice(start + j, start + j + 128)
                pieces = []
                for index_ref, z_ref in ((left_ref, zr_ref), (right_ref, zl_ref)):
                    u = h[:, j : j + 128] * z_ref[s, :, at]
                    group = jnp.broadcast_to(index_ref[0:1, at], (rows, 128)) >> 6
                    pieces += [jnp.where(group == a, u, 0.0) for a in range(groups)]
                u_ref[:, at] = jnp.concatenate(pieces, 0).astype(jnp.bfloat16)
        acc = jnp.dot(u_ref[...], hot_ref[...], preferred_element_type=jnp.float32)
        half = groups * rows
        left = [acc[a * rows : (a + 1) * rows, :64] for a in range(groups)]
        right = [acc[half + a * rows : half + (a + 1) * rows, 64:] for a in range(groups)]
        return jnp.concatenate(left, 1) + jnp.concatenate(right, 1)

    k1 = derive(state, 0, fetches)
    keep_ref[0] = state
    keep_ref[1] = state + 0.5 * DT * k1

    def section(s, total_slope):
        k = derive(keep_ref[s], s)

        @pl.when(s < 3)
        def _():
            keep_ref[s + 1] = state + jnp.where(s == 2, DT, 0.5 * DT) * k

        return total_slope + jnp.where(s == 3, 1.0, 2.0) * k

    slope = lax.fori_loop(1, 4, section, k1) / 6.0
    a = (state + DT * slope - target_ref[...]) / segments
    keep_ref[7] = DT / 6.0 * a
    hot_copy.wait()

    def back(t, carry):
        s = 3 - t
        c = pull(keep_ref[4 + s], s)
        keep_ref[3 + s] = jnp.where(s == 1, DT / 6.0, DT / 3.0) * a + jnp.where(s == 3, DT, 0.5 * DT) * c
        return carry

    lax.fori_loop(0, 3, back, 0)
    high = slope.astype(jnp.bfloat16).astype(jnp.float32)
    packed = jnp.concatenate([keep_ref[i] for i in range(8)] + [high, slope - high], 0).astype(jnp.bfloat16)
    for d in range(out_ref.shape[0]):
        out_ref[d] = packed


def run_chain(state, target, left, right, coeffs, hot, copies, segments):
    total, modes = coeffs.shape
    rows = state.shape[0]
    return pl.pallas_call(
        functools.partial(chain_kernel, 1.0 / math.sqrt(total), segments),
        out_shape=jax.ShapeDtypeStruct((copies, 10 * rows, modes), jnp.bfloat16),
        in_specs=[FULL] * 4 + [pl.BlockSpec(memory_space=pl.ANY)] * 2,
        out_specs=FULL,
        scratch_shapes=[
            pltpu.VMEM((total, modes), jnp.bfloat16),
            pltpu.VMEM((total, 128), jnp.bfloat16),
            pltpu.VMEM((4, rows, total), jnp.float32),
            pltpu.VMEM((4, rows, total), jnp.float32),
            pltpu.VMEM((2 * (modes // 64) * rows, total), jnp.bfloat16),
            pltpu.VMEM((8, rows, modes), jnp.float32),
            pltpu.SemaphoreType.DMA((total // CHUNK + 1,)),
        ],
        compiler_params=pltpu.CompilerParams(vmem_limit_bytes=56 * 2**20),
        name="chain",
    )(state, target, left, right, coeffs, hot)


def grad_kernel(scale, block, packed_ref, left_ref, right_ref, consts_ref, out_ref):
    count, height, modes = packed_ref.shape
    rows = height // 10
    y = packed_ref[:, : 4 * rows, :].reshape(count * 4 * rows, modes)
    g = packed_ref[:, 4 * rows : 8 * rows, :].reshape(count * 4 * rows, modes)
    cands = left_ref.shape[0]
    for start in range(0, cands, block):
        at = slice(start, start + block)
        zl = lax.dot_general(left_ref[at, :], y, NT, preferred_element_type=jnp.float32) + consts_ref[at, 0:1]
        zr = lax.dot_general(right_ref[at, :], y, NT, preferred_element_type=jnp.float32) + consts_ref[at, 1:2]
        theta = (zl * zr).astype(jnp.bfloat16)
        grad = scale * jnp.dot(theta, g, preferred_element_type=jnp.float32)
        out_ref[at, :] = grad.astype(jnp.bfloat16)
    rest = out_ref.shape[0] - cands
    out_ref[cands:, :] = jnp.zeros((rest, modes), jnp.bfloat16)


def run_grad(packed, left, right, consts, total, height):
    modes = packed.shape[2]
    return pl.pallas_call(
        functools.partial(grad_kernel, 1.0 / math.sqrt(total), 416),
        out_shape=jax.ShapeDtypeStruct((height, modes), jnp.bfloat16),
        in_specs=[FULL] * 4,
        out_specs=FULL,
        compiler_params=pltpu.CompilerParams(vmem_limit_bytes=32 * 2**20),
        name="grad",
    )(packed, left, right, consts)


def body(state, target, coeffs, pairs, mask):
    block_rows, modes = state.shape
    own = coeffs.shape[0]
    n_traj, n_cand = lax.axis_size("traj"), lax.axis_size("cand")
    segments, total = block_rows * n_traj, own * n_cand
    rows = block_rows // n_cand
    start = lax.axis_index("cand") * rows

    weights = lax.all_gather(coeffs, "cand", axis=0, tiled=True)
    index = lax.all_gather(pairs, "cand", axis=1, tiled=True)
    state_own = lax.dynamic_slice_in_dim(state, start, rows, 0)
    target_own = lax.dynamic_slice_in_dim(target, start, rows, 0)
    mode = jnp.arange(modes, dtype=jnp.int32)
    left_hot = (pairs[0][:, None] == mode[None, :]).astype(jnp.bfloat16)
    right_hot = (pairs[1][:, None] == mode[None, :]).astype(jnp.bfloat16)
    consts = (pairs.T == modes).astype(jnp.float32)
    piece = -(-own // (8 * n_traj)) * 8
    height = piece * n_traj
    at = lax.axis_index("traj") * piece
    fill = ((0, height - own), (0, 0))
    coeffs_piece = lax.dynamic_slice_in_dim(jnp.pad(coeffs, fill), at, piece, 0).astype(jnp.float32)
    mask_piece = lax.dynamic_slice_in_dim(jnp.pad(mask, fill), at, piece, 0).astype(jnp.float32)

    lane = jnp.arange(128, dtype=jnp.int32)[None, :]
    low = jnp.where(lane < 64, index[0][:, None], index[1][:, None]) & 63
    hot = (low == (lane & 63)).astype(jnp.bfloat16)

    packed = run_chain(state_own, target_own, index[0:1], index[1:2], weights, hot, n_cand, segments)
    packed = lax.all_to_all(packed, "cand", 0, 0, tiled=True)
    tail = packed[:, 8 * rows :, :].astype(jnp.float32)
    slope = (tail[:, :rows] + tail[:, rows:]).reshape(block_rows, modes)

    grad = run_grad(packed, left_hot, right_hot, consts, total, height)
    grad = lax.all_to_all(grad.reshape(n_traj, piece, modes), "traj", 0, 0, tiled=True)
    grad = jnp.sum(grad.astype(jnp.float32), axis=0)
    rate = 0.5 * math.sqrt(segments * total) / DT
    fresh = (mask_piece * (coeffs_piece - rate * grad)).astype(jnp.bfloat16)
    fresh = jnp.broadcast_to(fresh[None], (n_traj, piece, modes))
    fresh = lax.all_to_all(fresh, "traj", 0, 0, tiled=True)
    return slope, fresh.reshape(height, modes)[:own]


def solution(mesh):
    placed = (P("traj", None), P("traj", None), P("cand", None), P(None, "cand"), P("cand", None))
    return jax.shard_map(
        body,
        mesh=mesh,
        in_specs=placed,
        out_specs=(P("traj", None), P("cand", None)),
        check_vma=False,
    )
```

```python
import functools
import math

import jax
import jax.numpy as jnp
from jax import lax
from jax.experimental import pallas as pl
from jax.experimental.pallas import tpu as pltpu
from jax.sharding import Mesh, PartitionSpec as P

DT = 0.25
NT = (((1,), (1,)), ((), ()))
CHUNK = 1664
AXES = ("x", "y", "z", "c")
FULL = pl.BlockSpec(memory_space=pltpu.VMEM)


def chain_kernel(
    scale,
    segments,
    state_ref,
    target_ref,
    left_ref,
    right_ref,
    w_hbm,
    hot_hbm,
    out_ref,
    w_ref,
    hot_ref,
    zl_ref,
    zr_ref,
    u_ref,
    keep_ref,
    sems,
):
    rows, modes = state_ref.shape
    total = w_ref.shape[0]
    groups = modes // 64

    def fetch(start):
        at = pl.ds(start, CHUNK)
        return pltpu.make_async_copy(w_hbm.at[at], w_ref.at[at], sems.at[start // CHUNK])

    fetches = [fetch(start) for start in range(0, total, CHUNK)]
    for copy in fetches:
        copy.start()
    hot_copy = pltpu.make_async_copy(hot_hbm, hot_ref, sems.at[total // CHUNK])
    hot_copy.start()
    state = state_ref[...]

    def derive(y, s, waits=None):
        halves = [y[:, j : j + 128] for j in range(0, modes, 128)]

        def pick(index):
            index = jnp.broadcast_to(index, (rows, 128))
            lane = index & 127
            value = jnp.ones((rows, 128), jnp.float32)
            for j in reversed(range(len(halves))):
                value = jnp.where(index < 128 * (j + 1), jnp.take_along_axis(halves[j], lane, axis=1), value)
            return value

        acc = jnp.zeros((rows, modes), jnp.float32)
        for start in range(0, total, CHUNK):
            parts = []
            for j in range(start, start + CHUNK, 128):
                zl, zr = pick(left_ref[0:1, j : j + 128]), pick(right_ref[0:1, j : j + 128])
                zl_ref[s, :, j : j + 128] = zl
                zr_ref[s, :, j : j + 128] = zr
                parts.append((zl * zr).astype(jnp.bfloat16))
            theta = jnp.concatenate(parts, axis=1)
            if waits is not None:
                waits[start // CHUNK].wait()
            acc = acc + jnp.dot(theta, w_ref[start : start + CHUNK, :], preferred_element_type=jnp.float32)
        return scale * acc

    def pull(g, s):
        g16 = g.astype(jnp.bfloat16)
        for start in range(0, total, CHUNK):
            w = w_ref[start : start + CHUNK, :]
            h = scale * lax.dot_general(g16, w, NT, preferred_element_type=jnp.float32)
            for j in range(0, CHUNK, 128):
                at = slice(start + j, start + j + 128)
                pieces = []
                for index_ref, z_ref in ((left_ref, zr_ref), (right_ref, zl_ref)):
                    u = h[:, j : j + 128] * z_ref[s, :, at]
                    group = jnp.broadcast_to(index_ref[0:1, at], (rows, 128)) >> 6
                    pieces += [jnp.where(group == a, u, 0.0) for a in range(groups)]
                u_ref[:, at] = jnp.concatenate(pieces, 0).astype(jnp.bfloat16)
        acc = jnp.dot(u_ref[...], hot_ref[...], preferred_element_type=jnp.float32)
        half = groups * rows
        left = [acc[a * rows : (a + 1) * rows, :64] for a in range(groups)]
        right = [acc[half + a * rows : half + (a + 1) * rows, 64:] for a in range(groups)]
        return jnp.concatenate(left, 1) + jnp.concatenate(right, 1)

    k1 = derive(state, 0, fetches)
    keep_ref[0] = state
    keep_ref[1] = state + 0.5 * DT * k1

    def section(s, total_slope):
        k = derive(keep_ref[s], s)

        @pl.when(s < 3)
        def _():
            keep_ref[s + 1] = state + jnp.where(s == 2, DT, 0.5 * DT) * k

        return total_slope + jnp.where(s == 3, 1.0, 2.0) * k

    slope = lax.fori_loop(1, 4, section, k1) / 6.0
    a = (state + DT * slope - target_ref[...]) / segments
    keep_ref[7] = DT / 6.0 * a
    hot_copy.wait()

    def back(t, carry):
        s = 3 - t
        c = pull(keep_ref[4 + s], s)
        keep_ref[3 + s] = jnp.where(s == 1, DT / 6.0, DT / 3.0) * a + jnp.where(s == 3, DT, 0.5 * DT) * c
        return carry

    lax.fori_loop(0, 3, back, 0)
    packed = jnp.concatenate([slope] + [keep_ref[i] for i in range(1, 8)], 0).astype(jnp.bfloat16)
    for d in range(out_ref.shape[0]):
        out_ref[d] = packed


def run_chain(state, target, left, right, coeffs, hot, copies, segments):
    total, modes = coeffs.shape
    rows = state.shape[0]
    return pl.pallas_call(
        functools.partial(chain_kernel, 1.0 / math.sqrt(total), segments),
        out_shape=jax.ShapeDtypeStruct((copies, 8 * rows, modes), jnp.bfloat16),
        in_specs=[FULL] * 4 + [pl.BlockSpec(memory_space=pl.ANY)] * 2,
        out_specs=FULL,
        scratch_shapes=[
            pltpu.VMEM((total, modes), jnp.bfloat16),
            pltpu.VMEM((total, 128), jnp.bfloat16),
            pltpu.VMEM((4, rows, total), jnp.float32),
            pltpu.VMEM((4, rows, total), jnp.float32),
            pltpu.VMEM((2 * (modes // 64) * rows, total), jnp.bfloat16),
            pltpu.VMEM((8, rows, modes), jnp.float32),
            pltpu.SemaphoreType.DMA((total // CHUNK + 1,)),
        ],
        compiler_params=pltpu.CompilerParams(vmem_limit_bytes=56 * 2**20),
        name="chain",
    )(state, target, left, right, coeffs, hot)


def grad_kernel(scale, block, first_ref, mine_ref, other_ref, left_ref, right_ref, consts_ref, out_ref):
    count, height, modes = mine_ref.shape
    rows = height // 8
    ys, gs = [], []
    for core, ref in enumerate((mine_ref, other_ref)):
        values = ref[...].astype(jnp.float32)
        y = jnp.concatenate([first_ref[core], values[:, rows : 4 * rows]], 1)
        ys.append(y.reshape(count * 4 * rows, modes).astype(jnp.bfloat16))
        gs.append(values[:, 4 * rows :].reshape(count * 4 * rows, modes).astype(jnp.bfloat16))
    y, g = jnp.concatenate(ys, 0), jnp.concatenate(gs, 0)
    cands = left_ref.shape[0]
    for start in range(0, cands, block):
        at = slice(start, start + block)
        zl = lax.dot_general(left_ref[at, :], y, NT, preferred_element_type=jnp.float32) + consts_ref[at, 0:1]
        zr = lax.dot_general(right_ref[at, :], y, NT, preferred_element_type=jnp.float32) + consts_ref[at, 1:2]
        theta = (zl * zr).astype(jnp.bfloat16)
        grad = scale * jnp.dot(theta, g, preferred_element_type=jnp.float32)
        out_ref[at, :] = grad.astype(jnp.bfloat16)
    rest = out_ref.shape[0] - cands
    out_ref[cands:, :] = jnp.zeros((rest, modes), jnp.bfloat16)


def run_grad(first, mine, other, left, right, consts, total, height):
    modes = mine.shape[2]
    return pl.pallas_call(
        functools.partial(grad_kernel, 1.0 / math.sqrt(total), 416),
        out_shape=jax.ShapeDtypeStruct((height, modes), jnp.bfloat16),
        in_specs=[FULL] * 6,
        out_specs=FULL,
        compiler_params=pltpu.CompilerParams(vmem_limit_bytes=32 * 2**20),
        name="grad",
    )(first, mine, other, left, right, consts)


def exchange(blocks, axis):
    return lax.all_to_all(blocks, axis, 0, 0, tiled=True)


def spread(block, axis):
    count = lax.axis_size(axis)
    blocks = exchange(jnp.broadcast_to(block[None], (count, *block.shape)), axis)
    return blocks.reshape(count * block.shape[0], *block.shape[1:])


def body(state, target, coeffs, pairs, mask):
    block_rows, modes = state.shape
    own = coeffs.shape[0]
    nx, ny, nz, nc = [lax.axis_size(axis) for axis in AXES]
    segments, total = block_rows * nx * ny, own * nz * nc
    rows = block_rows // (nz * nc)
    core = lax.axis_index("c")
    start = lax.axis_index(("z", "c")) * rows

    weights = lax.all_gather(coeffs, ("z", "c"), axis=0, tiled=True)
    index = lax.all_gather(pairs, ("z", "c"), axis=1, tiled=True)
    state_own = lax.dynamic_slice_in_dim(state, start, rows, 0)
    target_own = lax.dynamic_slice_in_dim(target, start, rows, 0)
    lane = jnp.arange(128, dtype=jnp.int32)[None, :]
    low = jnp.where(lane < 64, index[0][:, None], index[1][:, None]) & 63
    hot = (low == (lane & 63)).astype(jnp.bfloat16)
    mode = jnp.arange(modes, dtype=jnp.int32)
    left_hot = (pairs[0][:, None] == mode[None, :]).astype(jnp.bfloat16)
    right_hot = (pairs[1][:, None] == mode[None, :]).astype(jnp.bfloat16)
    consts = (pairs.T == modes).astype(jnp.float32)
    by_core = state.reshape(nz, nc, rows, modes)
    first = jnp.where(core == 0, by_core[:, 0], by_core[:, 1]), jnp.where(core == 0, by_core[:, 1], by_core[:, 0])
    first = jnp.stack(first)
    piece = -(-own // (8 * nx * ny)) * 8
    height = piece * nx * ny
    at = lax.axis_index(("x", "y")) * piece
    fill = ((0, height - own), (0, 0))
    coeffs_piece = lax.dynamic_slice_in_dim(jnp.pad(coeffs, fill), at, piece, 0).astype(jnp.float32)
    mask_piece = lax.dynamic_slice_in_dim(jnp.pad(mask, fill), at, piece, 0).astype(jnp.float32)

    packed = run_chain(state_own, target_own, index[0:1], index[1:2], weights, hot, nz, segments)
    mine = exchange(packed, "z")
    other = lax.ppermute(mine, "c", [(0, 1), (1, 0)])
    grad = run_grad(first, mine, other, left_hot, right_hot, consts, total, height)

    slopes = [block[:, :rows].astype(jnp.float32) for block in (mine, other)]
    slope = jnp.stack([jnp.where(core == 0, *slopes), jnp.where(core == 0, *slopes[::-1])], 1)
    slope = slope.reshape(block_rows, modes)

    grad = exchange(grad.reshape(nx, ny * piece, modes), "x")
    grad = jnp.sum(grad.astype(jnp.float32), axis=0).astype(jnp.bfloat16)
    grad = exchange(grad.reshape(ny, piece, modes), "y")
    grad = jnp.sum(grad.astype(jnp.float32), axis=0)
    rate = 0.5 * math.sqrt(segments * total) / DT
    fresh = (mask_piece * (coeffs_piece - rate * grad)).astype(jnp.bfloat16)
    fresh = spread(spread(fresh, "y"), "x")
    return slope, fresh[:own]


def solution(mesh):
    devices = mesh.devices.reshape(4, 8, 8, 2)
    traj, cand = ("x", "y"), ("z", "c")
    placed = (P(traj, None), P(traj, None), P(cand, None), P(None, cand), P(cand, None))
    return jax.shard_map(
        body,
        mesh=Mesh(devices, AXES),
        in_specs=placed,
        out_specs=(P(traj, None), P(cand, None)),
        check_vma=False,
    )
```

```python
import functools
import math

import jax
import jax.numpy as jnp
from jax import lax
from jax.experimental import pallas as pl
from jax.experimental.pallas import tpu as pltpu
from jax.sharding import Mesh, PartitionSpec as P

DT = 0.25
NT = (((1,), (1,)), ((), ()))
CHUNK = 1664
FETCH = 2048
PIECE = 256
AXES = ("x", "y", "z", "c")
FULL = pl.BlockSpec(memory_space=pltpu.VMEM)


def chain_kernel(scale, segments, buffers, state_ref, target_ref, left_ref, right_ref, hot_hbm, *refs):
    blocks, (out_ref, w_ref, hot_ref, zl_ref, zr_ref, u_ref, keep_ref, sems) = refs[:buffers], refs[buffers:]
    rows, modes = state_ref.shape
    total = w_ref.shape[0]
    groups = modes // 64

    fetches, ends, base = [], [], 0
    for block in blocks:
        for start in range(0, block.shape[0], FETCH):
            size = min(FETCH, block.shape[0] - start)
            source, into = block.at[pl.ds(start, size)], w_ref.at[pl.ds(base + start, size)]
            fetches.append(pltpu.make_async_copy(source, into, sems.at[len(fetches)]))
            ends.append(base + start + size)
        base += block.shape[0]
    for copy in fetches:
        copy.start()
    hot_copy = pltpu.make_async_copy(hot_hbm, hot_ref, sems.at[len(fetches)])
    hot_copy.start()
    state = state_ref[...]

    def derive(y, s, waits=None):
        halves = [y[:, j : j + 128] for j in range(0, modes, 128)]

        def pick(index):
            index = jnp.broadcast_to(index, (rows, 128))
            lane = index & 127
            value = jnp.ones((rows, 128), jnp.float32)
            for j in reversed(range(len(halves))):
                value = jnp.where(index < 128 * (j + 1), jnp.take_along_axis(halves[j], lane, axis=1), value)
            return value

        acc = jnp.zeros((rows, modes), jnp.float32)
        for start in range(0, total, CHUNK):
            parts = []
            for j in range(start, start + CHUNK, 128):
                zl, zr = pick(left_ref[0:1, j : j + 128]), pick(right_ref[0:1, j : j + 128])
                zl_ref[s, :, j : j + 128] = zl
                zr_ref[s, :, j : j + 128] = zr
                parts.append((zl * zr).astype(jnp.bfloat16))
            theta = jnp.concatenate(parts, axis=1)
            while waits and ends[len(fetches) - len(waits)] - FETCH < start + CHUNK:
                waits.pop(0).wait()
            acc = acc + jnp.dot(theta, w_ref[start : start + CHUNK, :], preferred_element_type=jnp.float32)
        return scale * acc

    def pull(g, s):
        g16 = g.astype(jnp.bfloat16)
        for start in range(0, total, CHUNK):
            w = w_ref[start : start + CHUNK, :]
            h = scale * lax.dot_general(g16, w, NT, preferred_element_type=jnp.float32)
            for j in range(0, CHUNK, 128):
                at = slice(start + j, start + j + 128)
                pieces = []
                for index_ref, z_ref in ((left_ref, zr_ref), (right_ref, zl_ref)):
                    u = h[:, j : j + 128] * z_ref[s, :, at]
                    group = jnp.broadcast_to(index_ref[0:1, at], (rows, 128)) >> 6
                    pieces += [jnp.where(group == a, u, 0.0) for a in range(groups)]
                u_ref[:, at] = jnp.concatenate(pieces, 0).astype(jnp.bfloat16)
        acc = jnp.dot(u_ref[...], hot_ref[...], preferred_element_type=jnp.float32)
        half = groups * rows
        left = [acc[a * rows : (a + 1) * rows, :64] for a in range(groups)]
        right = [acc[half + a * rows : half + (a + 1) * rows, 64:] for a in range(groups)]
        return jnp.concatenate(left, 1) + jnp.concatenate(right, 1)

    k1 = derive(state, 0, list(fetches))
    keep_ref[0] = state
    keep_ref[1] = state + 0.5 * DT * k1

    def section(s, total_slope):
        k = derive(keep_ref[s], s)

        @pl.when(s < 3)
        def _():
            keep_ref[s + 1] = state + jnp.where(s == 2, DT, 0.5 * DT) * k

        return total_slope + jnp.where(s == 3, 1.0, 2.0) * k

    slope = lax.fori_loop(1, 4, section, k1) / 6.0
    a = (state + DT * slope - target_ref[...]) / segments
    keep_ref[7] = DT / 6.0 * a
    hot_copy.wait()

    def back(t, carry):
        s = 3 - t
        c = pull(keep_ref[4 + s], s)
        keep_ref[3 + s] = jnp.where(s == 1, DT / 6.0, DT / 3.0) * a + jnp.where(s == 3, DT, 0.5 * DT) * c
        return carry

    lax.fori_loop(0, 3, back, 0)
    packed = jnp.concatenate([slope] + [keep_ref[i] for i in range(1, 8)], 0).astype(jnp.bfloat16)
    for d in range(out_ref.shape[0]):
        out_ref[d] = packed


def run_chain(state, target, left, right, hot, blocks, copies, segments):
    total, modes = hot.shape[0], state.shape[1]
    rows = state.shape[0]
    copies_in = sum(-(-block.shape[0] // FETCH) for block in blocks)
    return pl.pallas_call(
        functools.partial(chain_kernel, 1.0 / math.sqrt(total), segments, len(blocks)),
        out_shape=jax.ShapeDtypeStruct((copies, 8 * rows, modes), jnp.bfloat16),
        in_specs=[FULL] * 4 + [pl.BlockSpec(memory_space=pl.ANY)] * (1 + len(blocks)),
        out_specs=FULL,
        scratch_shapes=[
            pltpu.VMEM((total, modes), jnp.bfloat16),
            pltpu.VMEM((total, 128), jnp.bfloat16),
            pltpu.VMEM((4, rows, total), jnp.float32),
            pltpu.VMEM((4, rows, total), jnp.float32),
            pltpu.VMEM((2 * (modes // 64) * rows, total), jnp.bfloat16),
            pltpu.VMEM((8, rows, modes), jnp.float32),
            pltpu.SemaphoreType.DMA((copies_in + 1,)),
        ],
        compiler_params=pltpu.CompilerParams(vmem_limit_bytes=56 * 2**20),
        name="chain",
    )(state, target, left, right, hot, *blocks)


def grad_kernel(scale, block, first_ref, mine_ref, other_ref, left_ref, right_ref, consts_ref, out_ref):
    count, height, modes = mine_ref.shape
    rows = height // 8
    ys, gs = [], []
    for core, ref in enumerate((mine_ref, other_ref)):
        values = ref[...].astype(jnp.float32)
        y = jnp.concatenate([first_ref[core], values[:, rows : 4 * rows]], 1)
        ys.append(y.reshape(count * 4 * rows, modes).astype(jnp.bfloat16))
        gs.append(values[:, 4 * rows :].reshape(count * 4 * rows, modes).astype(jnp.bfloat16))
    y, g = jnp.concatenate(ys, 0), jnp.concatenate(gs, 0)
    cands = left_ref.shape[0]
    for start in range(0, cands, block):
        at = slice(start, start + block)
        zl = lax.dot_general(left_ref[at, :], y, NT, preferred_element_type=jnp.float32) + consts_ref[at, 0:1]
        zr = lax.dot_general(right_ref[at, :], y, NT, preferred_element_type=jnp.float32) + consts_ref[at, 1:2]
        theta = (zl * zr).astype(jnp.bfloat16)
        grad = scale * jnp.dot(theta, g, preferred_element_type=jnp.float32)
        out_ref[at, :] = grad.astype(jnp.bfloat16)
    rest = out_ref.shape[0] - cands
    out_ref[cands:, :] = jnp.zeros((rest, modes), jnp.bfloat16)


def run_grad(first, mine, other, left, right, consts, total, height):
    modes = mine.shape[2]
    return pl.pallas_call(
        functools.partial(grad_kernel, 1.0 / math.sqrt(total), 416),
        out_shape=jax.ShapeDtypeStruct((height, modes), jnp.bfloat16),
        in_specs=[FULL] * 6,
        out_specs=FULL,
        compiler_params=pltpu.CompilerParams(vmem_limit_bytes=32 * 2**20),
        name="grad",
    )(first, mine, other, left, right, consts)


def gather_candidates(coeffs, pairs):
    nx, nz, nc = [lax.axis_size(axis) for axis in ("x", "z", "c")]
    cands, side = nz * nc, PIECE * nx
    x, core = lax.axis_index("x"), lax.axis_index("c")
    ahead = [(i, (i + 1) % nx) for i in range(nx)]
    behind = [(i, (i - 1) % nx) for i in range(nx)]
    swap = [(0, 1), (1, 0)]

    mine = lax.all_gather(lax.dynamic_slice_in_dim(coeffs, x * PIECE, PIECE, 0), ("z", "c"), axis=0, tiled=True)
    rest = lax.all_gather(coeffs[side:], ("z", "c"), axis=0, tiled=True)
    half = mine.shape[0] // 2
    part = lax.dynamic_slice_in_dim(mine, core * half, half, 0)
    one, three = lax.ppermute(part, "x", ahead), lax.ppermute(part, "x", behind)
    two = [lax.ppermute(one[: half // 2], "x", ahead), lax.ppermute(three[half // 2 :], "x", behind)]
    got = [one, three, *two]
    blocks = [rest, mine, *got, *[lax.ppermute(block, "c", swap) for block in got]]

    index = lax.all_gather(pairs, ("z", "c"), axis=1, tiled=True).reshape(2, cands, -1)
    sides = index[:, :, :side].reshape(2, cands, nx, PIECE)

    def piece(away, first, count):
        which = lax.rem(x + away, nx)
        return lax.dynamic_slice(sides, (0, first, which, 0), (2, count, 1, PIECE)).reshape(2, count * PIECE)

    order = [index[:, :, side:].reshape(2, -1), piece(0, 0, cands)]
    for first in (core * (cands // 2), (1 - core) * (cands // 2)):
        order += [piece(nx - 1, first, cands // 2), piece(1, first, cands // 2)]
        order += [piece(2, first, cands // 4), piece(2, first + cands // 4, cands // 4)]
    return blocks, jnp.concatenate(order, 1)


def exchange(blocks, axis):
    return lax.all_to_all(blocks, axis, 0, 0, tiled=True)


def spread(block, axis):
    count = lax.axis_size(axis)
    blocks = exchange(jnp.broadcast_to(block[None], (count, *block.shape)), axis)
    return blocks.reshape(count * block.shape[0], *block.shape[1:])


def body(state, target, coeffs, pairs, mask):
    block_rows, modes = state.shape
    own = coeffs.shape[0]
    nx, ny, nz, nc = [lax.axis_size(axis) for axis in AXES]
    segments, total = block_rows * nx * ny, own * nz * nc
    rows = block_rows // (nz * nc)
    core = lax.axis_index("c")
    start = lax.axis_index(("z", "c")) * rows

    blocks, index = gather_candidates(coeffs, pairs)
    state_own = lax.dynamic_slice_in_dim(state, start, rows, 0)
    target_own = lax.dynamic_slice_in_dim(target, start, rows, 0)
    lane = jnp.arange(128, dtype=jnp.int32)[None, :]
    low = jnp.where(lane < 64, index[0][:, None], index[1][:, None]) & 63
    hot = (low == (lane & 63)).astype(jnp.bfloat16)
    mode = jnp.arange(modes, dtype=jnp.int32)
    left_hot = (pairs[0][:, None] == mode[None, :]).astype(jnp.bfloat16)
    right_hot = (pairs[1][:, None] == mode[None, :]).astype(jnp.bfloat16)
    consts = (pairs.T == modes).astype(jnp.float32)
    by_core = state.reshape(nz, nc, rows, modes)
    first = jnp.where(core == 0, by_core[:, 0], by_core[:, 1]), jnp.where(core == 0, by_core[:, 1], by_core[:, 0])
    first = jnp.stack(first)
    piece = -(-own // (8 * nx * ny)) * 8
    height = piece * nx * ny
    at = lax.axis_index(("x", "y")) * piece
    fill = ((0, height - own), (0, 0))
    coeffs_piece = lax.dynamic_slice_in_dim(jnp.pad(coeffs, fill), at, piece, 0).astype(jnp.float32)
    mask_piece = lax.dynamic_slice_in_dim(jnp.pad(mask, fill), at, piece, 0).astype(jnp.float32)

    packed = run_chain(state_own, target_own, index[0:1], index[1:2], hot, blocks, nz, segments)
    mine = exchange(packed, "z")
    other = lax.ppermute(mine, "c", [(0, 1), (1, 0)])
    grad = run_grad(first, mine, other, left_hot, right_hot, consts, total, height)

    slopes = [block[:, :rows].astype(jnp.float32) for block in (mine, other)]
    slope = jnp.stack([jnp.where(core == 0, *slopes), jnp.where(core == 0, *slopes[::-1])], 1)
    slope = slope.reshape(block_rows, modes)

    grad = exchange(grad.reshape(nx, ny * piece, modes), "x")
    grad = jnp.sum(grad.astype(jnp.float32), axis=0).astype(jnp.bfloat16)
    grad = exchange(grad.reshape(ny, piece, modes), "y")
    grad = jnp.sum(grad.astype(jnp.float32), axis=0)
    rate = 0.5 * math.sqrt(segments * total) / DT
    fresh = (mask_piece * (coeffs_piece - rate * grad)).astype(jnp.bfloat16)
    fresh = spread(spread(fresh, "y"), "x")
    return slope, fresh[:own]


def solution(mesh):
    devices = mesh.devices.reshape(4, 8, 8, 2)
    traj, cand = ("x", "y"), ("z", "c")
    placed = (P(traj, None), P(traj, None), P(cand, None), P(None, cand), P(cand, None))
    return jax.shard_map(
        body,
        mesh=Mesh(devices, AXES),
        in_specs=placed,
        out_specs=(P(traj, None), P(cand, None)),
        check_vma=False,
    )
```

```python
import functools
import math

import jax
import jax.numpy as jnp
from jax import lax
from jax.experimental import pallas as pl
from jax.experimental.pallas import tpu as pltpu
from jax.sharding import Mesh, PartitionSpec as P

DT = 0.25
NT = (((1,), (1,)), ((), ()))
CHUNK = 1664
FETCH = 2048
PIECE = 64
AXES = ("x", "y", "z", "c")
FULL = pl.BlockSpec(memory_space=pltpu.VMEM)


def chain_kernel(scale, segments, buffers, state_ref, target_ref, left_ref, right_ref, hot_hbm, *refs):
    blocks, (out_ref, w_ref, hot_ref, zl_ref, zr_ref, u_ref, keep_ref, sems) = refs[:buffers], refs[buffers:]
    rows, modes = state_ref.shape
    total = w_ref.shape[0]
    groups = modes // 64

    fetches, ends, base = [], [], 0
    for block in blocks:
        for start in range(0, block.shape[0], FETCH):
            size = min(FETCH, block.shape[0] - start)
            source, into = block.at[pl.ds(start, size)], w_ref.at[pl.ds(base + start, size)]
            fetches.append(pltpu.make_async_copy(source, into, sems.at[len(fetches)]))
            ends.append(base + start + size)
        base += block.shape[0]
    for copy in fetches:
        copy.start()
    hot_copy = pltpu.make_async_copy(hot_hbm, hot_ref, sems.at[len(fetches)])
    state = state_ref[...]

    def derive(y, s, waits=None):
        halves = [y[:, j : j + 128] for j in range(0, modes, 128)]

        def pick(index):
            index = jnp.broadcast_to(index, (rows, 128))
            lane = index & 127
            value = jnp.ones((rows, 128), jnp.float32)
            for j in reversed(range(len(halves))):
                value = jnp.where(index < 128 * (j + 1), jnp.take_along_axis(halves[j], lane, axis=1), value)
            return value

        acc = jnp.zeros((rows, modes), jnp.float32)
        for start in range(0, total, CHUNK):
            parts = []
            for j in range(start, start + CHUNK, 128):
                zl, zr = pick(left_ref[0:1, j : j + 128]), pick(right_ref[0:1, j : j + 128])
                zl_ref[s, :, j : j + 128] = zl
                zr_ref[s, :, j : j + 128] = zr
                parts.append((zl * zr).astype(jnp.bfloat16))
            theta = jnp.concatenate(parts, axis=1)
            while waits and ends[len(fetches) - len(waits)] - FETCH < start + CHUNK:
                waits.pop(0).wait()
            acc = acc + jnp.dot(theta, w_ref[start : start + CHUNK, :], preferred_element_type=jnp.float32)
        return scale * acc

    def pull(g, s):
        g16 = g.astype(jnp.bfloat16)
        for start in range(0, total, CHUNK):
            w = w_ref[start : start + CHUNK, :]
            h = scale * lax.dot_general(g16, w, NT, preferred_element_type=jnp.float32)
            for j in range(0, CHUNK, 128):
                at = slice(start + j, start + j + 128)
                pieces = []
                for index_ref, z_ref in ((left_ref, zr_ref), (right_ref, zl_ref)):
                    u = h[:, j : j + 128] * z_ref[s, :, at]
                    group = jnp.broadcast_to(index_ref[0:1, at], (rows, 128)) >> 6
                    pieces += [jnp.where(group == a, u, 0.0) for a in range(groups)]
                u_ref[:, at] = jnp.concatenate(pieces, 0).astype(jnp.bfloat16)
        acc = jnp.dot(u_ref[...], hot_ref[...], preferred_element_type=jnp.float32)
        half = groups * rows
        left = [acc[a * rows : (a + 1) * rows, :64] for a in range(groups)]
        right = [acc[half + a * rows : half + (a + 1) * rows, 64:] for a in range(groups)]
        return jnp.concatenate(left, 1) + jnp.concatenate(right, 1)

    k1 = derive(state, 0, list(fetches))
    hot_copy.start()
    keep_ref[0] = state
    keep_ref[1] = state + 0.5 * DT * k1

    def section(s, total_slope):
        k = derive(keep_ref[s], s)

        @pl.when(s < 3)
        def _():
            keep_ref[s + 1] = state + jnp.where(s == 2, DT, 0.5 * DT) * k

        return total_slope + jnp.where(s == 3, 1.0, 2.0) * k

    slope = lax.fori_loop(1, 4, section, k1) / 6.0
    a = (state + DT * slope - target_ref[...]) / segments
    keep_ref[7] = DT / 6.0 * a
    hot_copy.wait()

    def back(t, carry):
        s = 3 - t
        c = pull(keep_ref[4 + s], s)
        keep_ref[3 + s] = jnp.where(s == 1, DT / 6.0, DT / 3.0) * a + jnp.where(s == 3, DT, 0.5 * DT) * c
        return carry

    lax.fori_loop(0, 3, back, 0)
    packed = jnp.concatenate([slope] + [keep_ref[i] for i in range(1, 8)], 0).astype(jnp.bfloat16)
    for d in range(out_ref.shape[0]):
        out_ref[d] = packed


def run_chain(state, target, left, right, hot, blocks, copies, segments):
    total, modes = hot.shape[0], state.shape[1]
    rows = state.shape[0]
    copies_in = sum(-(-block.shape[0] // FETCH) for block in blocks)
    return pl.pallas_call(
        functools.partial(chain_kernel, 1.0 / math.sqrt(total), segments, len(blocks)),
        out_shape=jax.ShapeDtypeStruct((copies, 8 * rows, modes), jnp.bfloat16),
        in_specs=[FULL] * 4 + [pl.BlockSpec(memory_space=pl.ANY)] * (1 + len(blocks)),
        out_specs=FULL,
        scratch_shapes=[
            pltpu.VMEM((total, modes), jnp.bfloat16),
            pltpu.VMEM((total, 128), jnp.bfloat16),
            pltpu.VMEM((4, rows, total), jnp.float32),
            pltpu.VMEM((4, rows, total), jnp.float32),
            pltpu.VMEM((2 * (modes // 64) * rows, total), jnp.bfloat16),
            pltpu.VMEM((8, rows, modes), jnp.float32),
            pltpu.SemaphoreType.DMA((copies_in + 1,)),
        ],
        compiler_params=pltpu.CompilerParams(vmem_limit_bytes=56 * 2**20),
        name="chain",
    )(state, target, left, right, hot, *blocks)


def grad_kernel(scale, block, first_ref, mine_ref, other_ref, left_ref, right_ref, consts_ref, out_ref):
    count, height, modes = mine_ref.shape
    rows = height // 8
    ys, gs = [], []
    for core, ref in enumerate((mine_ref, other_ref)):
        values = ref[...].astype(jnp.float32)
        y = jnp.concatenate([first_ref[core], values[:, rows : 4 * rows]], 1)
        ys.append(y.reshape(count * 4 * rows, modes).astype(jnp.bfloat16))
        gs.append(values[:, 4 * rows :].reshape(count * 4 * rows, modes).astype(jnp.bfloat16))
    y, g = jnp.concatenate(ys, 0), jnp.concatenate(gs, 0)
    cands = left_ref.shape[0]
    for start in range(0, cands, block):
        at = slice(start, start + block)
        zl = lax.dot_general(left_ref[at, :], y, NT, preferred_element_type=jnp.float32) + consts_ref[at, 0:1]
        zr = lax.dot_general(right_ref[at, :], y, NT, preferred_element_type=jnp.float32) + consts_ref[at, 1:2]
        theta = (zl * zr).astype(jnp.bfloat16)
        grad = scale * jnp.dot(theta, g, preferred_element_type=jnp.float32)
        out_ref[at, :] = grad.astype(jnp.bfloat16)


def run_grad(first, mine, other, left, right, consts, total):
    modes = mine.shape[2]
    return pl.pallas_call(
        functools.partial(grad_kernel, 1.0 / math.sqrt(total), 416),
        out_shape=jax.ShapeDtypeStruct((left.shape[0], modes), jnp.bfloat16),
        in_specs=[FULL] * 6,
        out_specs=FULL,
        compiler_params=pltpu.CompilerParams(vmem_limit_bytes=32 * 2**20),
        name="grad",
    )(first, mine, other, left, right, consts)


def exchange(blocks, axis):
    return lax.all_to_all(blocks, axis, 0, 0, tiled=True)


def spread(block, axis, count):
    blocks = exchange(jnp.broadcast_to(block[None], (count, *block.shape)), axis)
    return blocks.reshape(count * block.shape[0], *block.shape[1:])


def gather_candidates(coeffs, pairs):
    ny, nz, nc = [lax.axis_size(axis) for axis in ("y", "z", "c")]
    side = PIECE * ny
    core = lax.axis_index("c")
    piece = lax.dynamic_slice_in_dim(coeffs, lax.axis_index("y") * PIECE, PIECE, 0)
    rest = lax.all_gather(coeffs[side:], ("z", "c"), axis=0, tiled=True)
    mine = spread(spread(piece, "z", nz), "y", ny)
    other = lax.ppermute(mine, "c", [(0, 1), (1, 0)])

    index = spread(pairs[None], ("z", "c"), nz * nc).reshape(nz, nc, 2, -1).transpose(2, 0, 1, 3)
    order = [index[..., side:].reshape(2, -1)]
    sides = index[..., :side].reshape(2, nz, nc, ny, PIECE)
    for which in (core, 1 - core):
        part = jnp.where(which == 0, sides[:, :, 0], sides[:, :, 1])
        order.append(part.transpose(0, 2, 1, 3).reshape(2, -1))
    return [rest, mine, other], jnp.concatenate(order, 1)


def body(state, target, coeffs, pairs, mask):
    block_rows, modes = state.shape
    own = coeffs.shape[0]
    nx, ny, nz, nc = [lax.axis_size(axis) for axis in AXES]
    segments, total = block_rows * nx * ny, own * nz * nc
    rows = block_rows // (nz * nc)
    core = lax.axis_index("c")
    start = lax.axis_index(("z", "c")) * rows

    blocks, index = gather_candidates(coeffs, pairs)
    state_own = lax.dynamic_slice_in_dim(state, start, rows, 0)
    target_own = lax.dynamic_slice_in_dim(target, start, rows, 0)
    lane = jnp.arange(128, dtype=jnp.int32)[None, :]
    low = jnp.where(lane < 64, index[0][:, None], index[1][:, None]) & 63
    hot = (low == (lane & 63)).astype(jnp.bfloat16)
    mode = jnp.arange(modes, dtype=jnp.int32)
    left_hot = (pairs[0][:, None] == mode[None, :]).astype(jnp.bfloat16)
    right_hot = (pairs[1][:, None] == mode[None, :]).astype(jnp.bfloat16)
    consts = (pairs.T == modes).astype(jnp.float32)
    by_core = state.reshape(nz, nc, rows, modes)
    first = jnp.where(core == 0, by_core[:, 0], by_core[:, 1]), jnp.where(core == 0, by_core[:, 1], by_core[:, 0])
    first = jnp.stack(first)
    quarter = own // nx
    piece = -(-quarter // (8 * ny)) * 8
    extra = piece * ny - quarter
    at = lax.axis_index("x") * quarter + lax.axis_index("y") * piece
    fill = ((0, extra), (0, 0))
    coeffs_piece = lax.dynamic_slice_in_dim(jnp.pad(coeffs, fill), at, piece, 0).astype(jnp.float32)
    mask_piece = lax.dynamic_slice_in_dim(jnp.pad(mask, fill), at, piece, 0).astype(jnp.float32)

    packed = run_chain(state_own, target_own, index[0:1], index[1:2], hot, blocks, nz, segments)
    mine = exchange(packed, "z")
    other = lax.ppermute(mine, "c", [(0, 1), (1, 0)])
    grad = run_grad(first, mine, other, left_hot, right_hot, consts, total)

    slopes = [block[:, :rows].astype(jnp.float32) for block in (mine, other)]
    slope = jnp.stack([jnp.where(core == 0, *slopes), jnp.where(core == 0, *slopes[::-1])], 1)
    slope = slope.reshape(block_rows, modes)

    grad = exchange(grad.reshape(nx, quarter, modes), "x")
    grad = jnp.pad(jnp.sum(grad.astype(jnp.float32), axis=0).astype(jnp.bfloat16), fill)
    grad = exchange(grad.reshape(ny, piece, modes), "y")
    grad = jnp.sum(grad.astype(jnp.float32), axis=0)
    rate = 0.5 * math.sqrt(segments * total) / DT
    fresh = (mask_piece * (coeffs_piece - rate * grad)).astype(jnp.bfloat16)
    fresh = spread(spread(fresh, "y", ny)[:quarter], "x", nx)
    return slope, fresh


def solution(mesh):
    devices = mesh.devices.reshape(4, 8, 8, 2)
    traj, cand = ("x", "y"), ("z", "c")
    placed = (P(traj, None), P(traj, None), P(cand, None), P(None, cand), P(cand, None))
    return jax.shard_map(
        body,
        mesh=Mesh(devices, AXES),
        in_specs=placed,
        out_specs=(P(traj, None), P(cand, None)),
        check_vma=False,
    )
```

```python
import functools
import math

import jax
import jax.numpy as jnp
from jax import lax
from jax.experimental import pallas as pl
from jax.experimental.pallas import tpu as pltpu
from jax.sharding import Mesh, PartitionSpec as P

DT = 0.25
NT = (((1,), (1,)), ((), ()))
CHUNK = 1664
FETCH = 2048
AXES = ("x", "y", "z", "c")
FULL = pl.BlockSpec(memory_space=pltpu.VMEM)


def chain_kernel(scale, segments, buffers, state_ref, target_ref, left_ref, right_ref, hot_hbm, *refs):
    blocks, (out_ref, w_ref, hot_ref, zl_ref, zr_ref, u_ref, keep_ref, sems) = refs[:buffers], refs[buffers:]
    rows, modes = state_ref.shape
    total = w_ref.shape[0]
    groups = modes // 64

    fetches, ends, base = [], [], 0
    for block in blocks:
        for start in range(0, block.shape[0], FETCH):
            size = min(FETCH, block.shape[0] - start)
            source, into = block.at[pl.ds(start, size)], w_ref.at[pl.ds(base + start, size)]
            fetches.append(pltpu.make_async_copy(source, into, sems.at[len(fetches)]))
            ends.append(base + start + size)
        base += block.shape[0]
    for copy in fetches:
        copy.start()
    hot_copy = pltpu.make_async_copy(hot_hbm, hot_ref, sems.at[len(fetches)])
    state = state_ref[...]

    def derive(y, s, waits=None):
        halves = [y[:, j : j + 128] for j in range(0, modes, 128)]

        def pick(index):
            index = jnp.broadcast_to(index, (rows, 128))
            lane = index & 127
            value = jnp.ones((rows, 128), jnp.float32)
            for j in reversed(range(len(halves))):
                value = jnp.where(index < 128 * (j + 1), jnp.take_along_axis(halves[j], lane, axis=1), value)
            return value

        acc = jnp.zeros((rows, modes), jnp.float32)
        for start in range(0, total, CHUNK):
            parts = []
            for j in range(start, start + CHUNK, 128):
                zl, zr = pick(left_ref[0:1, j : j + 128]), pick(right_ref[0:1, j : j + 128])
                zl_ref[s, :, j : j + 128] = zl
                zr_ref[s, :, j : j + 128] = zr
                parts.append((zl * zr).astype(jnp.bfloat16))
            theta = jnp.concatenate(parts, axis=1)
            while waits and ends[len(fetches) - len(waits)] - FETCH < start + CHUNK:
                waits.pop(0).wait()
            acc = acc + jnp.dot(theta, w_ref[start : start + CHUNK, :], preferred_element_type=jnp.float32)
        return scale * acc

    def pull(g, s):
        g16 = g.astype(jnp.bfloat16)
        for start in range(0, total, CHUNK):
            w = w_ref[start : start + CHUNK, :]
            h = scale * lax.dot_general(g16, w, NT, preferred_element_type=jnp.float32)
            for j in range(0, CHUNK, 128):
                at = slice(start + j, start + j + 128)
                pieces = []
                for index_ref, z_ref in ((left_ref, zr_ref), (right_ref, zl_ref)):
                    u = h[:, j : j + 128] * z_ref[s, :, at]
                    group = jnp.broadcast_to(index_ref[0:1, at], (rows, 128)) >> 6
                    pieces += [jnp.where(group == a, u, 0.0) for a in range(groups)]
                u_ref[:, at] = jnp.concatenate(pieces, 0).astype(jnp.bfloat16)
        acc = jnp.dot(u_ref[...], hot_ref[...], preferred_element_type=jnp.float32)
        half = groups * rows
        left = [acc[a * rows : (a + 1) * rows, :64] for a in range(groups)]
        right = [acc[half + a * rows : half + (a + 1) * rows, 64:] for a in range(groups)]
        return jnp.concatenate(left, 1) + jnp.concatenate(right, 1)

    k1 = derive(state, 0, list(fetches))
    hot_copy.start()
    keep_ref[0] = state
    keep_ref[1] = state + 0.5 * DT * k1

    def section(s, total_slope):
        k = derive(keep_ref[s], s)

        @pl.when(s < 3)
        def _():
            keep_ref[s + 1] = state + jnp.where(s == 2, DT, 0.5 * DT) * k

        return total_slope + jnp.where(s == 3, 1.0, 2.0) * k

    slope = lax.fori_loop(1, 4, section, k1) / 6.0
    a = (state + DT * slope - target_ref[...]) / segments
    keep_ref[7] = DT / 6.0 * a
    hot_copy.wait()

    def back(t, carry):
        s = 3 - t
        c = pull(keep_ref[4 + s], s)
        keep_ref[3 + s] = jnp.where(s == 1, DT / 6.0, DT / 3.0) * a + jnp.where(s == 3, DT, 0.5 * DT) * c
        return carry

    lax.fori_loop(0, 3, back, 0)
    packed = jnp.concatenate([slope] + [keep_ref[i] for i in range(1, 8)], 0).astype(jnp.bfloat16)
    for d in range(out_ref.shape[0]):
        out_ref[d] = packed


def run_chain(state, target, left, right, hot, blocks, copies, segments):
    total, modes = hot.shape[0], state.shape[1]
    rows = state.shape[0]
    copies_in = sum(-(-block.shape[0] // FETCH) for block in blocks)
    return pl.pallas_call(
        functools.partial(chain_kernel, 1.0 / math.sqrt(total), segments, len(blocks)),
        out_shape=jax.ShapeDtypeStruct((copies, 8 * rows, modes), jnp.bfloat16),
        in_specs=[FULL] * 4 + [pl.BlockSpec(memory_space=pl.ANY)] * (1 + len(blocks)),
        out_specs=FULL,
        scratch_shapes=[
            pltpu.VMEM((total, modes), jnp.bfloat16),
            pltpu.VMEM((total, 128), jnp.bfloat16),
            pltpu.VMEM((4, rows, total), jnp.float32),
            pltpu.VMEM((4, rows, total), jnp.float32),
            pltpu.VMEM((2 * (modes // 64) * rows, total), jnp.bfloat16),
            pltpu.VMEM((8, rows, modes), jnp.float32),
            pltpu.SemaphoreType.DMA((copies_in + 1,)),
        ],
        compiler_params=pltpu.CompilerParams(vmem_limit_bytes=56 * 2**20),
        name="chain",
    )(state, target, left, right, hot, *blocks)


def grad_kernel(scale, block, first_ref, mine_ref, other_ref, left_ref, right_ref, consts_ref, out_ref):
    count, height, modes = mine_ref.shape
    rows = height // 8
    ys, gs = [], []
    for core, ref in enumerate((mine_ref, other_ref)):
        values = ref[...].astype(jnp.float32)
        y = jnp.concatenate([first_ref[core], values[:, rows : 4 * rows]], 1)
        ys.append(y.reshape(count * 4 * rows, modes).astype(jnp.bfloat16))
        gs.append(values[:, 4 * rows :].reshape(count * 4 * rows, modes).astype(jnp.bfloat16))
    y, g = jnp.concatenate(ys, 0), jnp.concatenate(gs, 0)
    cands = left_ref.shape[0]
    for start in range(0, cands, block):
        at = slice(start, start + block)
        zl = lax.dot_general(left_ref[at, :], y, NT, preferred_element_type=jnp.float32) + consts_ref[at, 0:1]
        zr = lax.dot_general(right_ref[at, :], y, NT, preferred_element_type=jnp.float32) + consts_ref[at, 1:2]
        theta = (zl * zr).astype(jnp.bfloat16)
        grad = scale * jnp.dot(theta, g, preferred_element_type=jnp.float32)
        out_ref[at, :] = grad.astype(jnp.bfloat16)


def run_grad(first, mine, other, left, right, consts, total):
    modes = mine.shape[2]
    return pl.pallas_call(
        functools.partial(grad_kernel, 1.0 / math.sqrt(total), 416),
        out_shape=jax.ShapeDtypeStruct((left.shape[0], modes), jnp.bfloat16),
        in_specs=[FULL] * 6,
        out_specs=FULL,
        compiler_params=pltpu.CompilerParams(vmem_limit_bytes=32 * 2**20),
        name="grad",
    )(first, mine, other, left, right, consts)


def exchange(blocks, axis):
    return lax.all_to_all(blocks, axis, 0, 0, tiled=True)


def spread(block, axis, count):
    blocks = exchange(jnp.broadcast_to(block[None], (count, *block.shape)), axis)
    return blocks.reshape(count * block.shape[0], *block.shape[1:])


def body(state, target, coeffs, pairs, mask):
    block_rows, modes = state.shape
    own = coeffs.shape[0]
    nx, ny, nz, nc = [lax.axis_size(axis) for axis in AXES]
    segments, total = block_rows * nx * ny, own * nz * nc
    rows = block_rows // (nz * nc)
    core = lax.axis_index("c")
    start = lax.axis_index(("z", "c")) * rows

    weights = lax.all_gather(coeffs, ("z", "c"), axis=0, tiled=True)
    index = lax.all_gather(pairs, ("z", "c"), axis=1, tiled=True)
    state_own = lax.dynamic_slice_in_dim(state, start, rows, 0)
    target_own = lax.dynamic_slice_in_dim(target, start, rows, 0)
    lane = jnp.arange(128, dtype=jnp.int32)[None, :]
    low = jnp.where(lane < 64, index[0][:, None], index[1][:, None]) & 63
    hot = (low == (lane & 63)).astype(jnp.bfloat16)
    mode = jnp.arange(modes, dtype=jnp.int32)
    left_hot = (pairs[0][:, None] == mode[None, :]).astype(jnp.bfloat16)
    right_hot = (pairs[1][:, None] == mode[None, :]).astype(jnp.bfloat16)
    consts = (pairs.T == modes).astype(jnp.float32)
    by_core = state.reshape(nz, nc, rows, modes)
    first = jnp.where(core == 0, by_core[:, 0], by_core[:, 1]), jnp.where(core == 0, by_core[:, 1], by_core[:, 0])
    first = jnp.stack(first)
    quarter = own // nx
    piece = -(-quarter // (8 * ny)) * 8
    extra = piece * ny - quarter
    at = lax.axis_index("x") * quarter + lax.axis_index("y") * piece
    fill = ((0, extra), (0, 0))
    coeffs_piece = lax.dynamic_slice_in_dim(jnp.pad(coeffs, fill), at, piece, 0).astype(jnp.float32)
    mask_piece = lax.dynamic_slice_in_dim(jnp.pad(mask, fill), at, piece, 0).astype(jnp.float32)

    packed = run_chain(state_own, target_own, index[0:1], index[1:2], hot, [weights], nz, segments)
    mine = exchange(packed, "z")
    other = lax.ppermute(mine, "c", [(0, 1), (1, 0)])
    grad = run_grad(first, mine, other, left_hot, right_hot, consts, total)

    slopes = [block[:, :rows].astype(jnp.float32) for block in (mine, other)]
    slope = jnp.stack([jnp.where(core == 0, *slopes), jnp.where(core == 0, *slopes[::-1])], 1)
    slope = slope.reshape(block_rows, modes)

    grad = exchange(grad.reshape(nx, quarter, modes), "x")
    grad = jnp.pad(jnp.sum(grad.astype(jnp.float32), axis=0).astype(jnp.bfloat16), fill)
    grad = exchange(grad.reshape(ny, piece, modes), "y")
    grad = jnp.sum(grad.astype(jnp.float32), axis=0)
    rate = 0.5 * math.sqrt(segments * total) / DT
    fresh = (mask_piece * (coeffs_piece - rate * grad)).astype(jnp.bfloat16)
    fresh = spread(spread(fresh, "y", ny)[:quarter], "x", nx)
    return slope, fresh


def solution(mesh):
    devices = mesh.devices.reshape(4, 8, 8, 2)
    traj, cand = ("x", "y"), ("z", "c")
    placed = (P(traj, None), P(traj, None), P(cand, None), P(None, cand), P(cand, None))
    return jax.shard_map(
        body,
        mesh=Mesh(devices, AXES),
        in_specs=placed,
        out_specs=(P(traj, None), P(cand, None)),
        check_vma=False,
    )
```

```python
import functools
import math

import jax
import jax.numpy as jnp
from jax import lax
from jax.experimental import pallas as pl
from jax.experimental.pallas import tpu as pltpu
from jax.sharding import Mesh, PartitionSpec as P

DT = 0.25
NT = (((1,), (1,)), ((), ()))
CHUNK = 1664
FETCH = 2048
PIECE = 40
AXES = ("x", "y", "z", "c")
FULL = pl.BlockSpec(memory_space=pltpu.VMEM)


def chain_kernel(scale, segments, buffers, state_ref, target_ref, left_ref, right_ref, hot_hbm, *refs):
    blocks, (out_ref, w_ref, hot_ref, zl_ref, zr_ref, u_ref, keep_ref, sems) = refs[:buffers], refs[buffers:]
    rows, modes = state_ref.shape
    total = w_ref.shape[0]
    groups = modes // 64

    fetches, ends, base = [], [], 0
    for block in blocks:
        for start in range(0, block.shape[0], FETCH):
            size = min(FETCH, block.shape[0] - start)
            source, into = block.at[pl.ds(start, size)], w_ref.at[pl.ds(base + start, size)]
            fetches.append(pltpu.make_async_copy(source, into, sems.at[len(fetches)]))
            ends.append(base + start + size)
        base += block.shape[0]
    for copy in fetches:
        copy.start()
    hot_copy = pltpu.make_async_copy(hot_hbm, hot_ref, sems.at[len(fetches)])
    state = state_ref[...]

    def derive(y, s, waits=None):
        halves = [y[:, j : j + 128] for j in range(0, modes, 128)]

        def pick(index):
            index = jnp.broadcast_to(index, (rows, 128))
            lane = index & 127
            value = jnp.ones((rows, 128), jnp.float32)
            for j in reversed(range(len(halves))):
                value = jnp.where(index < 128 * (j + 1), jnp.take_along_axis(halves[j], lane, axis=1), value)
            return value

        acc = jnp.zeros((rows, modes), jnp.float32)
        for start in range(0, total, CHUNK):
            parts = []
            for j in range(start, start + CHUNK, 128):
                zl, zr = pick(left_ref[0:1, j : j + 128]), pick(right_ref[0:1, j : j + 128])
                zl_ref[s, :, j : j + 128] = zl
                zr_ref[s, :, j : j + 128] = zr
                parts.append((zl * zr).astype(jnp.bfloat16))
            theta = jnp.concatenate(parts, axis=1)
            while waits and ends[len(fetches) - len(waits)] - FETCH < start + CHUNK:
                waits.pop(0).wait()
            acc = acc + jnp.dot(theta, w_ref[start : start + CHUNK, :], preferred_element_type=jnp.float32)
        return scale * acc

    def pull(g, s):
        g16 = g.astype(jnp.bfloat16)
        for start in range(0, total, CHUNK):
            w = w_ref[start : start + CHUNK, :]
            h = scale * lax.dot_general(g16, w, NT, preferred_element_type=jnp.float32)
            for j in range(0, CHUNK, 128):
                at = slice(start + j, start + j + 128)
                pieces = []
                for index_ref, z_ref in ((left_ref, zr_ref), (right_ref, zl_ref)):
                    u = h[:, j : j + 128] * z_ref[s, :, at]
                    group = jnp.broadcast_to(index_ref[0:1, at], (rows, 128)) >> 6
                    pieces += [jnp.where(group == a, u, 0.0) for a in range(groups)]
                u_ref[:, at] = jnp.concatenate(pieces, 0).astype(jnp.bfloat16)
        acc = jnp.dot(u_ref[...], hot_ref[...], preferred_element_type=jnp.float32)
        half = groups * rows
        left = [acc[a * rows : (a + 1) * rows, :64] for a in range(groups)]
        right = [acc[half + a * rows : half + (a + 1) * rows, 64:] for a in range(groups)]
        return jnp.concatenate(left, 1) + jnp.concatenate(right, 1)

    k1 = derive(state, 0, list(fetches))
    hot_copy.start()
    keep_ref[0] = state
    keep_ref[1] = state + 0.5 * DT * k1

    def section(s, total_slope):
        k = derive(keep_ref[s], s)

        @pl.when(s < 3)
        def _():
            keep_ref[s + 1] = state + jnp.where(s == 2, DT, 0.5 * DT) * k

        return total_slope + jnp.where(s == 3, 1.0, 2.0) * k

    slope = lax.fori_loop(1, 4, section, k1) / 6.0
    a = (state + DT * slope - target_ref[...]) / segments
    keep_ref[7] = DT / 6.0 * a
    hot_copy.wait()

    def back(t, carry):
        s = 3 - t
        c = pull(keep_ref[4 + s], s)
        keep_ref[3 + s] = jnp.where(s == 1, DT / 6.0, DT / 3.0) * a + jnp.where(s == 3, DT, 0.5 * DT) * c
        return carry

    lax.fori_loop(0, 3, back, 0)
    packed = jnp.concatenate([slope] + [keep_ref[i] for i in range(1, 8)], 0).astype(jnp.bfloat16)
    for d in range(out_ref.shape[0]):
        out_ref[d] = packed


def run_chain(state, target, left, right, hot, blocks, copies, segments):
    total, modes = hot.shape[0], state.shape[1]
    rows = state.shape[0]
    copies_in = sum(-(-block.shape[0] // FETCH) for block in blocks)
    return pl.pallas_call(
        functools.partial(chain_kernel, 1.0 / math.sqrt(total), segments, len(blocks)),
        out_shape=jax.ShapeDtypeStruct((copies, 8 * rows, modes), jnp.bfloat16),
        in_specs=[FULL] * 4 + [pl.BlockSpec(memory_space=pl.ANY)] * (1 + len(blocks)),
        out_specs=FULL,
        scratch_shapes=[
            pltpu.VMEM((total, modes), jnp.bfloat16),
            pltpu.VMEM((total, 128), jnp.bfloat16),
            pltpu.VMEM((4, rows, total), jnp.float32),
            pltpu.VMEM((4, rows, total), jnp.float32),
            pltpu.VMEM((2 * (modes // 64) * rows, total), jnp.bfloat16),
            pltpu.VMEM((8, rows, modes), jnp.float32),
            pltpu.SemaphoreType.DMA((copies_in + 1,)),
        ],
        compiler_params=pltpu.CompilerParams(vmem_limit_bytes=56 * 2**20),
        name="chain",
    )(state, target, left, right, hot, *blocks)


def grad_kernel(scale, block, first_ref, mine_ref, other_ref, left_ref, right_ref, consts_ref, out_ref):
    count, height, modes = mine_ref.shape
    rows = height // 8
    ys, gs = [], []
    for core, ref in enumerate((mine_ref, other_ref)):
        values = ref[...].astype(jnp.float32)
        y = jnp.concatenate([first_ref[core], values[:, rows : 4 * rows]], 1)
        ys.append(y.reshape(count * 4 * rows, modes).astype(jnp.bfloat16))
        gs.append(values[:, 4 * rows :].reshape(count * 4 * rows, modes).astype(jnp.bfloat16))
    y, g = jnp.concatenate(ys, 0), jnp.concatenate(gs, 0)
    cands = left_ref.shape[0]
    for start in range(0, cands, block):
        at = slice(start, start + block)
        zl = lax.dot_general(left_ref[at, :], y, NT, preferred_element_type=jnp.float32) + consts_ref[at, 0:1]
        zr = lax.dot_general(right_ref[at, :], y, NT, preferred_element_type=jnp.float32) + consts_ref[at, 1:2]
        theta = (zl * zr).astype(jnp.bfloat16)
        grad = scale * jnp.dot(theta, g, preferred_element_type=jnp.float32)
        out_ref[at, :] = grad.astype(jnp.bfloat16)


def run_grad(first, mine, other, left, right, consts, total):
    modes = mine.shape[2]
    return pl.pallas_call(
        functools.partial(grad_kernel, 1.0 / math.sqrt(total), 416),
        out_shape=jax.ShapeDtypeStruct((left.shape[0], modes), jnp.bfloat16),
        in_specs=[FULL] * 6,
        out_specs=FULL,
        compiler_params=pltpu.CompilerParams(vmem_limit_bytes=32 * 2**20),
        name="grad",
    )(first, mine, other, left, right, consts)


def exchange(blocks, axis):
    return lax.all_to_all(blocks, axis, 0, 0, tiled=True)


def spread(block, axis, count):
    blocks = exchange(jnp.broadcast_to(block[None], (count, *block.shape)), axis)
    return blocks.reshape(count * block.shape[0], *block.shape[1:])


def gather_candidates(coeffs, pairs):
    ny, nz, nc = [lax.axis_size(axis) for axis in ("y", "z", "c")]
    side = PIECE * ny
    core = lax.axis_index("c")
    piece = lax.dynamic_slice_in_dim(coeffs, lax.axis_index("y") * PIECE, PIECE, 0)
    rest = lax.all_gather(coeffs[side:], ("z", "c"), axis=0, tiled=True)

    index = spread(pairs[None], ("z", "c"), nz * nc).reshape(nz, nc, 2, -1).transpose(2, 0, 1, 3)
    order = [index[..., side:].reshape(2, -1)]
    sides = index[..., :side].reshape(2, nz, nc, ny, PIECE)
    for which in (core, 1 - core):
        part = jnp.where(which == 0, sides[:, :, 0], sides[:, :, 1])
        order.append(part.transpose(0, 2, 1, 3).reshape(2, -1))
    index = jnp.concatenate(order, 1)
    lane = jnp.arange(128, dtype=jnp.int32)[None, :]
    low = jnp.where(lane < 64, index[0][:, None], index[1][:, None]) & 63
    hot = (low == (lane & 63)).astype(jnp.bfloat16)

    mine = spread(spread(piece, "z", nz), "y", ny)
    mine, hot = lax.optimization_barrier((mine, hot))
    other = lax.ppermute(mine, "c", [(0, 1), (1, 0)])
    return [rest, mine, other], index, hot


def body(state, target, coeffs, pairs, mask):
    block_rows, modes = state.shape
    own = coeffs.shape[0]
    nx, ny, nz, nc = [lax.axis_size(axis) for axis in AXES]
    segments, total = block_rows * nx * ny, own * nz * nc
    rows = block_rows // (nz * nc)
    core = lax.axis_index("c")
    start = lax.axis_index(("z", "c")) * rows

    blocks, index, hot = gather_candidates(coeffs, pairs)
    state_own = lax.dynamic_slice_in_dim(state, start, rows, 0)
    target_own = lax.dynamic_slice_in_dim(target, start, rows, 0)
    mode = jnp.arange(modes, dtype=jnp.int32)
    left_hot = (pairs[0][:, None] == mode[None, :]).astype(jnp.bfloat16)
    right_hot = (pairs[1][:, None] == mode[None, :]).astype(jnp.bfloat16)
    consts = (pairs.T == modes).astype(jnp.float32)
    by_core = state.reshape(nz, nc, rows, modes)
    first = jnp.where(core == 0, by_core[:, 0], by_core[:, 1]), jnp.where(core == 0, by_core[:, 1], by_core[:, 0])
    first = jnp.stack(first)
    quarter = own // nx
    piece = -(-quarter // (8 * ny)) * 8
    extra = piece * ny - quarter
    at = lax.axis_index("x") * quarter + lax.axis_index("y") * piece
    fill = ((0, extra), (0, 0))
    coeffs_piece = lax.dynamic_slice_in_dim(jnp.pad(coeffs, fill), at, piece, 0).astype(jnp.float32)
    mask_piece = lax.dynamic_slice_in_dim(jnp.pad(mask, fill), at, piece, 0).astype(jnp.float32)

    packed = run_chain(state_own, target_own, index[0:1], index[1:2], hot, blocks, nz, segments)
    mine = exchange(packed, "z")
    other = lax.ppermute(mine, "c", [(0, 1), (1, 0)])
    grad = run_grad(first, mine, other, left_hot, right_hot, consts, total)

    slopes = [block[:, :rows].astype(jnp.float32) for block in (mine, other)]
    slope = jnp.stack([jnp.where(core == 0, *slopes), jnp.where(core == 0, *slopes[::-1])], 1)
    slope = slope.reshape(block_rows, modes)

    grad = exchange(grad.reshape(nx, quarter, modes), "x")
    grad = jnp.pad(jnp.sum(grad.astype(jnp.float32), axis=0).astype(jnp.bfloat16), fill)
    grad = exchange(grad.reshape(ny, piece, modes), "y")
    grad = jnp.sum(grad.astype(jnp.float32), axis=0)
    rate = 0.5 * math.sqrt(segments * total) / DT
    fresh = (mask_piece * (coeffs_piece - rate * grad)).astype(jnp.bfloat16)
    fresh = spread(spread(fresh, "y", ny)[:quarter], "x", nx)
    return slope, fresh


def solution(mesh):
    devices = mesh.devices.reshape(4, 8, 8, 2)
    traj, cand = ("x", "y"), ("z", "c")
    placed = (P(traj, None), P(traj, None), P(cand, None), P(None, cand), P(cand, None))
    return jax.shard_map(
        body,
        mesh=Mesh(devices, AXES),
        in_specs=placed,
        out_specs=(P(traj, None), P(cand, None)),
        check_vma=False,
    )
```

```python
import functools
import math

import jax
import jax.numpy as jnp
from jax import lax
from jax.experimental import pallas as pl
from jax.experimental.pallas import tpu as pltpu
from jax.sharding import Mesh, PartitionSpec as P

DT = 0.25
NT = (((1,), (1,)), ((), ()))
CHUNK = 1664
FETCH = 2048
PIECE = 48
AXES = ("x", "y", "z", "c")
FULL = pl.BlockSpec(memory_space=pltpu.VMEM)


def chain_kernel(scale, segments, buffers, state_ref, target_ref, left_ref, right_ref, hot_hbm, *refs):
    blocks, (out_ref, w_ref, hot_ref, zl_ref, zr_ref, u_ref, keep_ref, sems) = refs[:buffers], refs[buffers:]
    rows, modes = state_ref.shape
    total = w_ref.shape[0]
    groups = modes // 64

    fetches, ends, base = [], [], 0
    for block in blocks:
        for start in range(0, block.shape[0], FETCH):
            size = min(FETCH, block.shape[0] - start)
            source, into = block.at[pl.ds(start, size)], w_ref.at[pl.ds(base + start, size)]
            fetches.append(pltpu.make_async_copy(source, into, sems.at[len(fetches)]))
            ends.append(base + start + size)
        base += block.shape[0]
    for copy in fetches:
        copy.start()
    hot_copy = pltpu.make_async_copy(hot_hbm, hot_ref, sems.at[len(fetches)])
    state = state_ref[...]

    def derive(y, s, waits=None):
        halves = [y[:, j : j + 128] for j in range(0, modes, 128)]

        def pick(index):
            index = jnp.broadcast_to(index, (rows, 128))
            lane = index & 127
            value = jnp.ones((rows, 128), jnp.float32)
            for j in reversed(range(len(halves))):
                value = jnp.where(index < 128 * (j + 1), jnp.take_along_axis(halves[j], lane, axis=1), value)
            return value

        acc = jnp.zeros((rows, modes), jnp.float32)
        for start in range(0, total, CHUNK):
            parts = []
            for j in range(start, start + CHUNK, 128):
                zl, zr = pick(left_ref[0:1, j : j + 128]), pick(right_ref[0:1, j : j + 128])
                zl_ref[s, :, j : j + 128] = zl
                zr_ref[s, :, j : j + 128] = zr
                parts.append((zl * zr).astype(jnp.bfloat16))
            theta = jnp.concatenate(parts, axis=1)
            while waits and ends[len(fetches) - len(waits)] - FETCH < start + CHUNK:
                waits.pop(0).wait()
            acc = acc + jnp.dot(theta, w_ref[start : start + CHUNK, :], preferred_element_type=jnp.float32)
        return scale * acc

    def pull(g, s):
        g16 = g.astype(jnp.bfloat16)
        for start in range(0, total, CHUNK):
            w = w_ref[start : start + CHUNK, :]
            h = scale * lax.dot_general(g16, w, NT, preferred_element_type=jnp.float32)
            for j in range(0, CHUNK, 128):
                at = slice(start + j, start + j + 128)
                pieces = []
                for index_ref, z_ref in ((left_ref, zr_ref), (right_ref, zl_ref)):
                    u = h[:, j : j + 128] * z_ref[s, :, at]
                    group = jnp.broadcast_to(index_ref[0:1, at], (rows, 128)) >> 6
                    pieces += [jnp.where(group == a, u, 0.0) for a in range(groups)]
                u_ref[:, at] = jnp.concatenate(pieces, 0).astype(jnp.bfloat16)
        acc = jnp.dot(u_ref[...], hot_ref[...], preferred_element_type=jnp.float32)
        half = groups * rows
        left = [acc[a * rows : (a + 1) * rows, :64] for a in range(groups)]
        right = [acc[half + a * rows : half + (a + 1) * rows, 64:] for a in range(groups)]
        return jnp.concatenate(left, 1) + jnp.concatenate(right, 1)

    k1 = derive(state, 0, list(fetches))
    hot_copy.start()
    keep_ref[0] = state
    keep_ref[1] = state + 0.5 * DT * k1

    def section(s, total_slope):
        k = derive(keep_ref[s], s)

        @pl.when(s < 3)
        def _():
            keep_ref[s + 1] = state + jnp.where(s == 2, DT, 0.5 * DT) * k

        return total_slope + jnp.where(s == 3, 1.0, 2.0) * k

    slope = lax.fori_loop(1, 4, section, k1) / 6.0
    a = (state + DT * slope - target_ref[...]) / segments
    keep_ref[7] = DT / 6.0 * a
    hot_copy.wait()

    def back(t, carry):
        s = 3 - t
        c = pull(keep_ref[4 + s], s)
        keep_ref[3 + s] = jnp.where(s == 1, DT / 6.0, DT / 3.0) * a + jnp.where(s == 3, DT, 0.5 * DT) * c
        return carry

    lax.fori_loop(0, 3, back, 0)
    packed = jnp.concatenate([slope] + [keep_ref[i] for i in range(1, 8)], 0).astype(jnp.bfloat16)
    for d in range(out_ref.shape[0]):
        out_ref[d] = packed


def run_chain(state, target, left, right, hot, blocks, copies, segments):
    total, modes = hot.shape[0], state.shape[1]
    rows = state.shape[0]
    copies_in = sum(-(-block.shape[0] // FETCH) for block in blocks)
    return pl.pallas_call(
        functools.partial(chain_kernel, 1.0 / math.sqrt(total), segments, len(blocks)),
        out_shape=jax.ShapeDtypeStruct((copies, 8 * rows, modes), jnp.bfloat16),
        in_specs=[FULL] * 4 + [pl.BlockSpec(memory_space=pl.ANY)] * (1 + len(blocks)),
        out_specs=FULL,
        scratch_shapes=[
            pltpu.VMEM((total, modes), jnp.bfloat16),
            pltpu.VMEM((total, 128), jnp.bfloat16),
            pltpu.VMEM((4, rows, total), jnp.float32),
            pltpu.VMEM((4, rows, total), jnp.float32),
            pltpu.VMEM((2 * (modes // 64) * rows, total), jnp.bfloat16),
            pltpu.VMEM((8, rows, modes), jnp.float32),
            pltpu.SemaphoreType.DMA((copies_in + 1,)),
        ],
        compiler_params=pltpu.CompilerParams(vmem_limit_bytes=56 * 2**20),
        name="chain",
    )(state, target, left, right, hot, *blocks)


def grad_kernel(scale, block, first_ref, mine_ref, other_ref, left_ref, right_ref, consts_ref, out_ref):
    count, height, modes = mine_ref.shape
    rows = height // 8
    ys, gs = [], []
    for core, ref in enumerate((mine_ref, other_ref)):
        values = ref[...].astype(jnp.float32)
        y = jnp.concatenate([first_ref[core], values[:, rows : 4 * rows]], 1)
        ys.append(y.reshape(count * 4 * rows, modes).astype(jnp.bfloat16))
        gs.append(values[:, 4 * rows :].reshape(count * 4 * rows, modes).astype(jnp.bfloat16))
    y, g = jnp.concatenate(ys, 0), jnp.concatenate(gs, 0)
    cands = left_ref.shape[0]
    for start in range(0, cands, block):
        at = slice(start, start + block)
        zl = lax.dot_general(left_ref[at, :], y, NT, preferred_element_type=jnp.float32) + consts_ref[at, 0:1]
        zr = lax.dot_general(right_ref[at, :], y, NT, preferred_element_type=jnp.float32) + consts_ref[at, 1:2]
        theta = (zl * zr).astype(jnp.bfloat16)
        grad = scale * jnp.dot(theta, g, preferred_element_type=jnp.float32)
        out_ref[at, :] = grad.astype(jnp.bfloat16)


def run_grad(first, mine, other, left, right, consts, total):
    modes = mine.shape[2]
    return pl.pallas_call(
        functools.partial(grad_kernel, 1.0 / math.sqrt(total), 416),
        out_shape=jax.ShapeDtypeStruct((left.shape[0], modes), jnp.bfloat16),
        in_specs=[FULL] * 6,
        out_specs=FULL,
        compiler_params=pltpu.CompilerParams(vmem_limit_bytes=32 * 2**20),
        name="grad",
    )(first, mine, other, left, right, consts)


def exchange(blocks, axis):
    return lax.all_to_all(blocks, axis, 0, 0, tiled=True)


def spread(block, axis, count):
    blocks = exchange(jnp.broadcast_to(block[None], (count, *block.shape)), axis)
    return blocks.reshape(count * block.shape[0], *block.shape[1:])


def gather_candidates(coeffs, pairs):
    ny, nz, nc = [lax.axis_size(axis) for axis in ("y", "z", "c")]
    side = PIECE * ny
    core = lax.axis_index("c")
    piece = lax.dynamic_slice_in_dim(coeffs, lax.axis_index("y") * PIECE, PIECE, 0)
    rest = lax.all_gather(coeffs[side:], ("z", "c"), axis=0, tiled=True)

    index = spread(pairs[None], ("z", "c"), nz * nc).reshape(nz, nc, 2, -1).transpose(2, 0, 1, 3)
    order = [index[..., side:].reshape(2, -1)]
    sides = index[..., :side].reshape(2, nz, nc, ny, PIECE)
    for which in (core, 1 - core):
        part = jnp.where(which == 0, sides[:, :, 0], sides[:, :, 1])
        order.append(part.transpose(0, 2, 1, 3).reshape(2, -1))
    index = jnp.concatenate(order, 1)
    lane = jnp.arange(128, dtype=jnp.int32)[None, :]
    low = jnp.where(lane < 64, index[0][:, None], index[1][:, None]) & 63
    hot = (low == (lane & 63)).astype(jnp.bfloat16)

    mine = spread(spread(piece, "z", nz), "y", ny)
    mine, hot = lax.optimization_barrier((mine, hot))
    other = lax.ppermute(mine, "c", [(0, 1), (1, 0)])
    return [rest, mine, other], index, hot


def body(state, target, coeffs, pairs, mask):
    block_rows, modes = state.shape
    own = coeffs.shape[0]
    nx, ny, nz, nc = [lax.axis_size(axis) for axis in AXES]
    segments, total = block_rows * nx * ny, own * nz * nc
    rows = block_rows // (nz * nc)
    core = lax.axis_index("c")
    start = lax.axis_index(("z", "c")) * rows

    blocks, index, hot = gather_candidates(coeffs, pairs)
    state_own = lax.dynamic_slice_in_dim(state, start, rows, 0)
    target_own = lax.dynamic_slice_in_dim(target, start, rows, 0)
    mode = jnp.arange(modes, dtype=jnp.int32)
    left_hot = (pairs[0][:, None] == mode[None, :]).astype(jnp.bfloat16)
    right_hot = (pairs[1][:, None] == mode[None, :]).astype(jnp.bfloat16)
    consts = (pairs.T == modes).astype(jnp.float32)
    by_core = state.reshape(nz, nc, rows, modes)
    first = jnp.where(core == 0, by_core[:, 0], by_core[:, 1]), jnp.where(core == 0, by_core[:, 1], by_core[:, 0])
    first = jnp.stack(first)
    quarter = own // nx
    piece = -(-quarter // (8 * ny)) * 8
    extra = piece * ny - quarter
    at = lax.axis_index("x") * quarter + lax.axis_index("y") * piece
    fill = ((0, extra), (0, 0))
    coeffs_piece = lax.dynamic_slice_in_dim(jnp.pad(coeffs, fill), at, piece, 0).astype(jnp.float32)
    mask_piece = lax.dynamic_slice_in_dim(jnp.pad(mask, fill), at, piece, 0).astype(jnp.float32)

    packed = run_chain(state_own, target_own, index[0:1], index[1:2], hot, blocks, nz, segments)
    mine = exchange(packed, "z")
    other = lax.ppermute(mine, "c", [(0, 1), (1, 0)])
    grad = run_grad(first, mine, other, left_hot, right_hot, consts, total)

    slopes = [block[:, :rows].astype(jnp.float32) for block in (mine, other)]
    slope = jnp.stack([jnp.where(core == 0, *slopes), jnp.where(core == 0, *slopes[::-1])], 1)
    slope = slope.reshape(block_rows, modes)

    grad = exchange(grad.reshape(nx, quarter, modes), "x")
    grad = jnp.pad(jnp.sum(grad.astype(jnp.float32), axis=0).astype(jnp.bfloat16), fill)
    grad = exchange(grad.reshape(ny, piece, modes), "y")
    grad = jnp.sum(grad.astype(jnp.float32), axis=0)
    rate = 0.5 * math.sqrt(segments * total) / DT
    fresh = (mask_piece * (coeffs_piece - rate * grad)).astype(jnp.bfloat16)
    fresh = spread(spread(fresh, "y", ny)[:quarter], "x", nx)
    return slope, fresh


def solution(mesh):
    devices = mesh.devices.reshape(4, 8, 8, 2)
    traj, cand = ("x", "y"), ("z", "c")
    placed = (P(traj, None), P(traj, None), P(cand, None), P(None, cand), P(cand, None))
    return jax.shard_map(
        body,
        mesh=Mesh(devices, AXES),
        in_specs=placed,
        out_specs=(P(traj, None), P(cand, None)),
        check_vma=False,
    )
```
